32 devices in a mesh: chan: 8 (over z, x), freq: 4 (over y, core).
Axes of the slice: x: 2, y: 2, z: 4, core: 2. Of those that a mesh axis runs over, the one named last changes fastest.
Arguments:
- strain: bfloat16 [512, 256, 1024], P('chan', 'freq'), may hold values from -6 to 6
- mad_index: int32 [512], P('chan'), may hold values from 0 to 15
- mad_table: float32 [16], replicated, may hold values from 0.25 to 2.5
- freq_bins: int32 [64], replicated, may hold values from 1 to 511
- valid_count: int32 [512], P('chan'), may hold values from 64 to 256
Outputs:
- cross: float32 [64, 2, 512, 512], P('freq', None, 'chan')
The draws below stay inside these ranges and needn't reach their ends.
All inputs are finite; a program needn't handle non-finite values.
Results may differ from the reference program's by a relative error of at most 0.0057.
Values may be sent and summed in bfloat16 or wider, within the bound.
A program may use at most 256 MiB of HBM per device.

```python
import math
import jax
import jax.numpy as jnp
from jax import lax

L = 1024
NF = 64
NT = 16
CHANNELS = 512
WINDOWS = 256


def with_ends(drawn, rng, least, top_value):
    place = [jax.random.randint(jax.random.fold_in(rng, axis), (), 0, length) for axis, length in enumerate(drawn.shape)]
    widest = drawn.shape.index(max(drawn.shape))
    beside = place[:widest] + [(place[widest] + 1) % drawn.shape[widest]] + place[widest + 1:]
    return drawn.at[tuple(place)].set(least).at[tuple(beside)].set(top_value)


def steps_of(rng, shape, pieces, low, top_value):
    def one(axis_at, shards_of):
        draws = jax.random.uniform(jax.random.fold_in(jax.random.fold_in(rng, 6), axis_at), (shards_of,), jnp.float32, low / len(pieces), top_value / len(pieces))
        return jnp.repeat(jnp.exp(draws), shape[axis_at] // shards_of).reshape((-1,) + (1,) * (len(shape) - axis_at - 1))

    factor_of = one(*pieces[0])
    for cut in pieces[1:]:
        factor_of = factor_of * one(*cut)
    return factor_of


def noise(rng, extent, deviation, limit, pieces=(), kind=jnp.bfloat16):
    loudness = steps_of(rng, extent, pieces, -0.22, 0.18) if pieces else 1.0
    result = jax.random.normal(rng, extent, jnp.float32) * deviation * loudness
    return jnp.minimum(jnp.maximum(result, -limit), limit).astype(kind)


def setup_inputs(seed: int = 0) -> dict:
    key_of = jax.random.split(jax.random.key(seed), 6)
    return {
        "strain": noise(key_of[0], (CHANNELS, WINDOWS, L), 1.0, 6.0, ((0, 8), (1, 4))),
        "mad_index": with_ends(jax.random.randint(key_of[1], (CHANNELS,), 0, NT), jax.random.fold_in(key_of[1], 1), 0, NT - 1).astype(jnp.int32),
        "mad_table": jnp.clip(jnp.exp(jax.random.uniform(key_of[2], (NT,), jnp.float32, math.log(0.25), math.log(2.5))), 0.25, 2.5),
        "freq_bins": with_ends(jax.random.randint(key_of[3], (NF,), 1, L // 2), jax.random.fold_in(key_of[3], 1), 1, (L // 2) - 1).astype(jnp.int32),
        "valid_count": with_ends(jax.random.randint(key_of[4], (CHANNELS,), WINDOWS // 4, WINDOWS + 1), jax.random.fold_in(key_of[4], 1), WINDOWS // 4, WINDOWS).astype(jnp.int32),
    }


CLIP_FACTOR = 2.0

def dft_table(freq_bins, length):
    samples = jnp.arange(length, dtype=jnp.int32)
    phase_index = samples[:, None] * freq_bins[None, :] % length
    angle = phase_index.astype(jnp.float32) * (2.0 * math.pi / length)
    taper = 0.5 - 0.5 * jnp.cos(samples.astype(jnp.float32) * (2.0 * math.pi / length))
    cosine = taper[:, None] * jnp.cos(angle)
    sine = -taper[:, None] * jnp.sin(angle)
    stacked = jnp.stack([cosine, sine], axis=2)
    return stacked.reshape(length, 2 * freq_bins.shape[0]).astype(jnp.bfloat16)

def reference(strain, mad_index, mad_table, freq_bins, valid_count):
    channels, windows, length = strain.shape
    bin_count = freq_bins.shape[0]
    limits = mad_table[mad_index] * CLIP_FACTOR
    table = dft_table(freq_bins, length)

    def per_channel(inputs):
        rows_in, limit_one = inputs
        clipped = jnp.clip(rows_in.astype(jnp.float32), -limit_one, limit_one).astype(jnp.bfloat16)
        return jnp.dot(clipped, table, preferred_element_type=jnp.float32)
    spectrum = lax.map(per_channel, (strain, limits))
    window_ids = jnp.arange(windows, dtype=jnp.int32)
    counts = valid_count.astype(jnp.float32)
    weights = jnp.where(window_ids[None, :] < valid_count[:, None], 1.0 / jnp.sqrt(counts)[:, None], 0.0)
    weighted = (spectrum * weights[:, :, None]).astype(jnp.bfloat16)
    weighted = jnp.transpose(weighted.reshape(channels, windows, bin_count, 2), (2, 3, 0, 1))

    def per_bin(bin_panel):
        stacked = bin_panel.reshape(2 * channels, windows)
        products = jnp.dot(stacked, stacked.T, preferred_element_type=jnp.float32)
        real_part = products[:channels, :channels] + products[channels:, channels:]
        imag_part = products[channels:, :channels] - products[:channels, channels:]
        return jnp.stack([real_part, imag_part])
    return lax.map(per_bin, weighted)
```

```python
import functools
import math

import jax
import jax.numpy as jnp
from jax import lax
from jax.experimental import pallas as pl
from jax.experimental.pallas import tpu as pltpu
from jax.sharding import PartitionSpec as P

CLIP_FACTOR = 2.0
MESH = pl.DeviceIdType.MESH
PAIR = 2
BF16 = jnp.bfloat16
F32 = jnp.float32


def dft_rows(freq_bins, length):
    samples = jnp.arange(length, dtype=jnp.int32)
    phase_index = freq_bins[:, None] * samples[None, :] % length
    angle = phase_index.astype(F32) * (2.0 * math.pi / length)
    taper = 0.5 - 0.5 * jnp.cos(samples.astype(F32) * (2.0 * math.pi / length))
    cosine = taper[None, :] * jnp.cos(angle)
    sine = -taper[None, :] * jnp.sin(angle)
    return jnp.concatenate([cosine, sine], axis=0).astype(BF16)


def spectrum_kernel(limit_ref, count_ref, root_ref, table_ref, strain_ref, out_ref):
    block, wins, length = strain_ref.shape
    bins = out_ref.shape[1]
    first = pl.program_id(0) * block
    clipped = []
    for c in range(block):
        limit = jnp.full((wins, 128), limit_ref[first + c], F32).astype(BF16)
        limit = jnp.concatenate([limit] * (length // 128), axis=1)
        clipped.append(jnp.minimum(jnp.maximum(strain_ref[c], -limit), limit))
    rows = jnp.concatenate(clipped, axis=0)
    spectrum = lax.dot_general(
        table_ref[...], rows, (((1,), (1,)), ((), ())), preferred_element_type=F32
    )
    lane = lax.broadcasted_iota(jnp.int32, (bins, 2 * wins), 1)
    low = lane < wins
    window = lax.axis_index("freq") * wins + lax.rem(lane, wins)
    for c in range(0, block, 2):
        re = spectrum[:bins, c * wins : (c + 2) * wins]
        im = spectrum[bins:, c * wins : (c + 2) * wins]
        even = jnp.where(low, re, pltpu.roll(im, wins, 1))
        odd = jnp.where(low, pltpu.roll(re, wins, 1), im)
        for d, both in enumerate((even, odd)):
            channel = first + c + d
            weight = jnp.where(window < count_ref[channel], root_ref[channel], 0.0)
            out_ref[c + d] = (both * weight).astype(BF16)


def spectra(strain, limits, valid_count, roots, table):
    channels, wins, length = strain.shape
    bins = table.shape[0] // 2
    block = 8
    smem = pl.BlockSpec(memory_space=pltpu.SMEM)
    return pl.pallas_call(
        spectrum_kernel,
        grid=(channels // block,),
        out_shape=jax.ShapeDtypeStruct((channels, bins, 2 * wins), BF16),
        in_specs=[
            smem,
            smem,
            smem,
            pl.BlockSpec((2 * bins, length), lambda i: (0, 0)),
            pl.BlockSpec((block, wins, length), lambda i: (i, 0, 0)),
        ],
        out_specs=pl.BlockSpec((block, bins, 2 * wins), lambda i: (i, 0, 0)),
        compiler_params=pltpu.CompilerParams(vmem_limit_bytes=32 * 2**20),
    )(limits, valid_count, roots, table, strain)


def cross_kernel(groups, parts, w_ref, o_ref, panel, left, stage, own_sem, a_send, a_recv,
                 up_send, down_send, z_recv, r_send, r_recv):
    pieces = parts * PAIR
    bins, rows, lanes = panel.shape[2:]
    chan, q = lax.axis_index("chan"), lax.axis_index("freq")
    z, x = chan // PAIR, lax.rem(chan, PAIR)
    me = q * PAIR + x
    has_up, has_down = z < groups - 1, z > 0

    def place(piece):
        return (z * PAIR + lax.rem(piece, PAIR), piece // PAIR)

    above, below, mate = (chan + PAIR, q), (chan - PAIR, q), (z * PAIR + 1 - x, q)

    barrier = pltpu.get_barrier_semaphore()
    for d in range(1, pieces):
        pl.semaphore_signal(barrier, inc=1, device_id=place(lax.rem(me + d, pieces)), device_id_type=MESH)

    @pl.when(has_up)
    def _():
        pl.semaphore_signal(barrier, inc=1, device_id=above, device_id_type=MESH)

    @pl.when(has_down)
    def _():
        pl.semaphore_signal(barrier, inc=1, device_id=below, device_id_type=MESH)

    greeted = pieces - 1 + jnp.where(has_up, 1, 0) + jnp.where(has_down, 1, 0)
    pl.semaphore_wait(barrier, greeted)

    def swap(d):
        to = lax.rem(me + d, pieces)
        return pltpu.make_async_remote_copy(
            src_ref=w_ref.at[to], dst_ref=panel.at[z, me], send_sem=a_send.at[d],
            recv_sem=a_recv.at[d], device_id=place(to), device_id_type=MESH)

    def arrival(d):
        source = lax.rem(me + pieces - d, pieces)
        return source, pltpu.make_async_remote_copy(
            src_ref=w_ref.at[source], dst_ref=panel.at[z, source], send_sem=a_send.at[d],
            recv_sem=a_recv.at[d], device_id=place(source), device_id_type=MESH)

    def along(p, k, sems, target):
        return pltpu.make_async_remote_copy(
            src_ref=panel.at[p, k], dst_ref=panel.at[p, k], send_sem=sems.at[p, k],
            recv_sem=z_recv.at[p, k], device_id=target, device_id_type=MESH)

    def pass_up(p, k):
        @pl.when(has_up)
        def _():
            along(p, k, up_send, above).start()

    def pass_down(p, k):
        @pl.when(has_down)
        def _():
            along(p, k, down_send, below).start()

    own = pltpu.make_async_copy(w_ref.at[me], panel.at[z, me], own_sem)
    own.start()
    for d in range(1, pieces):
        swap(d).start()
    own.wait()
    pass_up(z, me)
    pass_down(z, me)
    for d in range(1, pieces):
        source, copy = arrival(d)
        copy.wait_recv()
        pass_up(z, source)
        pass_down(z, source)

    def wide(p, f):
        return jnp.concatenate(
            [
                jnp.concatenate([panel[p, part * PAIR + i, f] for i in range(PAIR)], axis=0)
                for part in range(parts)
            ],
            axis=1,
        )

    half = lanes // 2
    height = PAIR * rows

    @pl.loop(0, bins)
    def _(f):
        plain = wide(z, f)
        left[f, pl.ds(0, height)] = plain
        sign = jnp.where(lax.broadcasted_iota(jnp.int32, (height, lanes), 1) < half, 1.0, -1.0)
        for part in range(parts):
            turned = pltpu.roll(plain[:, part * lanes : (part + 1) * lanes].astype(F32), half, 1)
            left[f, pl.ds(height, height), pl.ds(part * lanes, lanes)] = (turned * sign).astype(BF16)

    def give_back(p):
        return pltpu.make_async_remote_copy(
            src_ref=stage.at[p],
            dst_ref=o_ref.at[pl.ds(x * bins, bins), :, :, pl.ds(pl.multiple_of(p * height, height), height)],
            send_sem=r_send.at[p], recv_sem=r_recv.at[p], device_id=mate, device_id_type=MESH)

    def get_back(p):
        return pltpu.make_async_remote_copy(
            src_ref=stage.at[p],
            dst_ref=o_ref.at[pl.ds((1 - x) * bins, bins), :, :, pl.ds(pl.multiple_of(p * height, height), height)],
            send_sem=r_send.at[p], recv_sem=r_recv.at[p], device_id=mate, device_id_type=MESH)

    def block(p):
        columns = pl.ds(pl.multiple_of(p * height, height), height)

        @pl.loop(0, bins)
        def _(f):
            product = lax.dot_general(
                left[f], wide(p, f), (((1,), (1,)), ((), ())), preferred_element_type=F32
            ).astype(BF16)
            for part in range(2):
                lower = product[part * height : part * height + rows]
                upper = product[part * height + rows : (part + 1) * height]
                first = x == 0
                o_ref[x * bins + f, part, :, columns] = jnp.where(first, lower, upper)
                stage[p, f, part] = jnp.where(first, upper, lower)

        give_back(p).start()

    block(z)

    def step(s, carry):
        lower, upper = z - 1 - s, z + 1 + s
        for k in range(pieces):
            @pl.when(lower >= 0)
            def _():
                along(lower, k, up_send, above).wait_recv()
                pass_up(lower, k)

            @pl.when(upper < groups)
            def _():
                along(upper, k, down_send, below).wait_recv()
                pass_down(upper, k)

        @pl.when(lower >= 0)
        def _():
            block(lower)

        @pl.when(upper < groups)
        def _():
            block(upper)

        return carry

    lax.fori_loop(0, groups - 1, step, 0)

    for d in range(1, pieces):
        swap(d).wait_send()

    def finish(p, carry):
        give_back(p).wait_send()
        get_back(p).wait_recv()
        for k in range(pieces):
            @pl.when(has_up & (p <= z))
            def _():
                along(p, k, up_send, above).wait_send()

            @pl.when(has_down & (p >= z))
            def _():
                along(p, k, down_send, below).wait_send()

        return carry

    lax.fori_loop(0, groups, finish, 0)


def cross(weighted, groups, parts):
    pieces, bins, rows, lanes = weighted.shape
    dma = pltpu.SemaphoreType.DMA
    return pl.pallas_call(
        functools.partial(cross_kernel, groups, parts),
        out_shape=jax.ShapeDtypeStruct((PAIR * bins, 2, rows, groups * PAIR * rows), BF16),
        in_specs=[pl.BlockSpec(memory_space=pl.ANY)],
        out_specs=pl.BlockSpec(memory_space=pltpu.VMEM),
        scratch_shapes=[
            pltpu.VMEM((groups, pieces, bins, rows, lanes), BF16),
            pltpu.VMEM((bins, 2 * PAIR * rows, parts * lanes), BF16),
            pltpu.VMEM((groups, bins, 2, rows, PAIR * rows), BF16),
            dma, dma((pieces,)), dma((pieces,)),
            dma((groups, pieces)), dma((groups, pieces)), dma((groups, pieces)),
            dma((groups,)), dma((groups,)),
        ],
        compiler_params=pltpu.CompilerParams(
            collective_id=0, has_side_effects=True, vmem_limit_bytes=56 * 2**20
        ),
    )(weighted)


def per_device(strain, mad_index, mad_table, freq_bins, valid_count):
    channels, wins, length = strain.shape
    bins = freq_bins.shape[0]
    entries = jnp.arange(mad_table.shape[0], dtype=jnp.int32)
    matches = mad_index[:, None] == entries[None, :]
    limits = jnp.sum(jnp.where(matches, mad_table[None, :], 0.0), axis=1) * CLIP_FACTOR
    roots = 1.0 / jnp.sqrt(valid_count.astype(F32))
    table = dft_rows(freq_bins, length)
    weighted = spectra(strain, limits, valid_count, roots, table)
    parts, groups = lax.axis_size("freq"), lax.axis_size("chan") // PAIR
    pieces = parts * PAIR
    weighted = jnp.transpose(weighted, (1, 0, 2)).reshape(pieces, bins // pieces, channels, 2 * wins)
    return cross(weighted, groups, parts).astype(F32)


def solution(mesh):
    return jax.shard_map(
        per_device,
        mesh=mesh,
        in_specs=(P("chan", "freq", None), P("chan"), P(), P(), P("chan")),
        out_specs=P("freq", None, "chan", None),
        check_vma=False,
    )
```

```python
import functools
import math

import jax
import jax.numpy as jnp
from jax import lax
from jax.experimental import pallas as pl
from jax.experimental.pallas import tpu as pltpu
from jax.sharding import PartitionSpec as P

CLIP_FACTOR = 2.0
MESH = pl.DeviceIdType.MESH
PAIR = 2
BF16 = jnp.bfloat16
F32 = jnp.float32


def dft_rows(freq_bins, length):
    samples = jnp.arange(length, dtype=jnp.int32)
    phase_index = freq_bins[:, None] * samples[None, :] % length
    angle = phase_index.astype(F32) * (2.0 * math.pi / length)
    taper = 0.5 - 0.5 * jnp.cos(samples.astype(F32) * (2.0 * math.pi / length))
    cosine = taper[None, :] * jnp.cos(angle)
    sine = -taper[None, :] * jnp.sin(angle)
    return jnp.concatenate([cosine, sine], axis=0).astype(BF16)


def spectrum_kernel(limit_ref, count_ref, root_ref, table_ref, strain_ref, out_ref):
    block, wins, length = strain_ref.shape
    bins = out_ref.shape[1]
    first = pl.program_id(0) * block
    clipped = []
    for c in range(block):
        limit = jnp.full((wins, 128), limit_ref[first + c], F32).astype(BF16)
        limit = jnp.concatenate([limit] * (length // 128), axis=1)
        clipped.append(jnp.minimum(jnp.maximum(strain_ref[c], -limit), limit))
    rows = jnp.concatenate(clipped, axis=0)
    spectrum = lax.dot_general(
        table_ref[...], rows, (((1,), (1,)), ((), ())), preferred_element_type=F32
    )
    lane = lax.broadcasted_iota(jnp.int32, (bins, 2 * wins), 1)
    low = lane < wins
    window = lax.axis_index("freq") * wins + lax.rem(lane, wins)
    for c in range(0, block, 2):
        re = spectrum[:bins, c * wins : (c + 2) * wins]
        im = spectrum[bins:, c * wins : (c + 2) * wins]
        even = jnp.where(low, re, pltpu.roll(im, wins, 1))
        odd = jnp.where(low, pltpu.roll(re, wins, 1), im)
        for d, both in enumerate((even, odd)):
            channel = first + c + d
            weight = jnp.where(window < count_ref[channel], root_ref[channel], 0.0)
            out_ref[c + d] = (both * weight).astype(BF16)


def spectra(strain, limits, valid_count, roots, table):
    channels, wins, length = strain.shape
    bins = table.shape[0] // 2
    block = 8
    smem = pl.BlockSpec(memory_space=pltpu.SMEM)
    return pl.pallas_call(
        spectrum_kernel,
        grid=(channels // block,),
        out_shape=jax.ShapeDtypeStruct((channels, bins, 2 * wins), BF16),
        in_specs=[
            smem,
            smem,
            smem,
            pl.BlockSpec((2 * bins, length), lambda i: (0, 0)),
            pl.BlockSpec((block, wins, length), lambda i: (i, 0, 0)),
        ],
        out_specs=pl.BlockSpec((block, bins, 2 * wins), lambda i: (i, 0, 0)),
        compiler_params=pltpu.CompilerParams(vmem_limit_bytes=60 * 2**20),
    )(limits, valid_count, roots, table, strain)


def cross_kernel(groups, parts, cuts, w_ref, o_ref, panel, left, left_end, stage, stage_end, own_sem, a_send,
                 a_recv, up_send, down_send, z_recv, r_send, r_recv, e_send, e_recv):
    pieces = parts * PAIR
    bins, rows, lanes = panel.shape[2:]
    cut = bins // cuts
    height = PAIR * rows
    half = lanes // 2
    last = groups - 1
    chan, q = lax.axis_index("chan"), lax.axis_index("freq")
    z, x = chan // PAIR, lax.rem(chan, PAIR)
    me = q * PAIR + x
    is_end = (z == 0) | (z == last)
    is_inner = (z > 0) & (z < last)
    low_pair, high_pair = (z == 1), (z == last - 1)
    is_helper = low_pair | high_pair
    end = jnp.where(low_pair, 0, last)
    sends_up, sends_down = z < last - 1, z > 1

    def place(piece):
        return (z * PAIR + lax.rem(piece, PAIR), piece // PAIR)

    def at(group, side):
        return (group * PAIR + side, q)

    above, below, mate = at(z + 1, x), at(z - 1, x), at(z, 1 - x)

    barrier = pltpu.get_barrier_semaphore()

    def greet(device):
        pl.semaphore_signal(barrier, inc=1, device_id=device, device_id_type=MESH)

    for d in range(1, pieces):
        greet(place(lax.rem(me + d, pieces)))

    @pl.when(z < last)
    def _():
        greet(above)

    @pl.when(z > 0)
    def _():
        greet(below)

    @pl.when((z == 0) | high_pair)
    def _():
        greet(at(z + 1, 1 - x))

    @pl.when((z == last) | low_pair)
    def _():
        greet(at(z - 1, 1 - x))

    greeted = pieces - 1 + jnp.where(z < last, 1, 0) + jnp.where(z > 0, 1, 0)
    greeted = greeted + jnp.where(is_end | is_helper, 1, 0)
    pl.semaphore_wait(barrier, greeted)

    def span(h):
        return pl.ds(h * cut, cut)

    def swap(d, h):
        to = lax.rem(me + d, pieces)
        return pltpu.make_async_remote_copy(
            src_ref=w_ref.at[to, span(h)], dst_ref=panel.at[z, me, span(h)], send_sem=a_send.at[d, h],
            recv_sem=a_recv.at[d, h], device_id=place(to), device_id_type=MESH)

    def arrival(d, h):
        source = lax.rem(me + pieces - d, pieces)
        return source, pltpu.make_async_remote_copy(
            src_ref=w_ref.at[source, span(h)], dst_ref=panel.at[z, source, span(h)], send_sem=a_send.at[d, h],
            recv_sem=a_recv.at[d, h], device_id=place(source), device_id_type=MESH)

    def along(p, k, h, sems, target):
        return pltpu.make_async_remote_copy(
            src_ref=panel.at[p, k, span(h)], dst_ref=panel.at[p, k, span(h)], send_sem=sems.at[p, k, h],
            recv_sem=z_recv.at[p, k, h], device_id=target, device_id_type=MESH)

    def pass_up(p, k, h):
        @pl.when(sends_up)
        def _():
            along(p, k, h, up_send, above).start()

    def pass_down(p, k, h):
        @pl.when(sends_down)
        def _():
            along(p, k, h, down_send, below).start()

    own = pltpu.make_async_copy(w_ref.at[me], panel.at[z, me], own_sem)
    own.start()
    for h in range(cuts):
        for d in range(1, pieces):
            swap(d, h).start()
    own.wait()

    def wide(p, f):
        return jnp.concatenate(
            [
                jnp.concatenate([panel[p, part * PAIR + i, f] for i in range(PAIR)], axis=0)
                for part in range(parts)
            ],
            axis=1,
        )

    def make_left(target, p, h):
        @pl.loop(0, cut)
        def _(i):
            f = h * cut + i
            plain = wide(p, f)
            target[f, pl.ds(0, height)] = plain
            sign = jnp.where(lax.broadcasted_iota(jnp.int32, (height, lanes), 1) < half, 1.0, -1.0)
            for part in range(parts):
                turned = pltpu.roll(plain[:, part * lanes : (part + 1) * lanes].astype(F32), half, 1)
                target[f, pl.ds(height, height), pl.ds(part * lanes, lanes)] = (turned * sign).astype(BF16)

    def columns(p):
        return pl.ds(pl.multiple_of(p * height, height), height)

    def give_back(p, h, side):
        return pltpu.make_async_remote_copy(
            src_ref=stage.at[p, span(h)],
            dst_ref=o_ref.at[pl.ds(side * bins + h * cut, cut), :, :, columns(p)],
            send_sem=r_send.at[p, h], recv_sem=r_recv.at[p, h], device_id=mate, device_id_type=MESH)

    def give_end(p, h, to, source):
        return pltpu.make_async_remote_copy(
            src_ref=stage_end.at[p, to, span(h)],
            dst_ref=o_ref.at[pl.ds(source * bins + h * cut, cut), :, :, columns(p)],
            send_sem=e_send.at[p, to, h], recv_sem=e_recv.at[p, source, h],
            device_id=at(end, to), device_id_type=MESH)

    def product_of(lhs, p, f):
        return lax.dot_general(
            lhs[f], wide(p, f), (((1,), (1,)), ((), ())), preferred_element_type=F32
        ).astype(BF16)

    def block(p, h):
        @pl.loop(0, cut)
        def _(i):
            f = h * cut + i
            product = product_of(left, p, f)
            for part in range(2):
                lower = product[part * height : part * height + rows]
                upper = product[part * height + rows : (part + 1) * height]
                o_ref[x * bins + f, part, :, columns(p)] = jnp.where(x == 0, lower, upper)
                stage[p, f, part] = jnp.where(x == 0, upper, lower)

        give_back(p, h, x).start()

    def block_end(p, h):
        @pl.loop(0, cut)
        def _(i):
            f = h * cut + i
            product = product_of(left_end, p, f)
            for part in range(2):
                for to in range(PAIR):
                    top = part * height + to * rows
                    stage_end[p, to, f, part] = product[top : top + rows]

        for to in range(PAIR):
            give_end(p, h, to, x).start()

    for h in range(cuts):
        pass_up(z, me, h)
        pass_down(z, me, h)
    for h in range(cuts):
        for d in range(1, pieces):
            source, copy = arrival(d, h)
            copy.wait_recv()
            pass_up(z, source, h)
            pass_down(z, source, h)
    for h in range(cuts):
        make_left(left, z, h)
        block(z, h)

    def step(s, carry):
        lower, upper = z - 1 - s, z + 1 + s
        for h in range(cuts):
            @pl.when(lower >= 0)
            def _():
                for k in range(pieces):
                    along(lower, k, h, up_send, above).wait_recv()
                    pass_up(lower, k, h)

            @pl.when(upper <= last)
            def _():
                for k in range(pieces):
                    along(upper, k, h, down_send, below).wait_recv()
                    pass_down(upper, k, h)

            @pl.when(is_helper & (s == 0))
            def _():
                make_left(left_end, end, h)
                block_end(z, h)

            @pl.when(is_helper & (lower > 0))
            def _():
                block_end(lower, h)

            @pl.when(is_helper & (upper < last))
            def _():
                block_end(upper, h)

            @pl.when(low_pair & (upper == last))
            def _():
                block_end(upper, h)

            @pl.when(high_pair & (lower == 0))
            def _():
                block_end(lower, h)

            @pl.when(lower >= 0)
            def _():
                block(lower, h)

            @pl.when(upper <= last)
            def _():
                block(upper, h)

        return carry

    @pl.when(is_inner)
    def _():
        lax.fori_loop(0, last, step, 0)

    for h in range(cuts):
        for d in range(1, pieces):
            swap(d, h).wait_send()

    def finish(p, carry):
        for h in range(cuts):
            @pl.when(is_inner | (p == z))
            def _():
                give_back(p, h, x).wait_send()
                give_back(p, h, 1 - x).wait_recv()

            @pl.when(is_end & (p != z))
            def _():
                for source in range(PAIR):
                    give_end(p, h, 0, source).wait_recv()

            @pl.when(is_helper & (p != end))
            def _():
                for to in range(PAIR):
                    give_end(p, h, to, x).wait_send()

            for k in range(pieces):
                @pl.when(sends_up & (p <= z))
                def _():
                    along(p, k, h, up_send, above).wait_send()

                @pl.when(sends_down & (p >= z))
                def _():
                    along(p, k, h, down_send, below).wait_send()

        return carry

    lax.fori_loop(0, groups, finish, 0)


def cross(weighted, groups, parts):
    assert groups >= 4
    pieces, bins, rows, lanes = weighted.shape
    cuts = 2
    dma = pltpu.SemaphoreType.DMA
    left = pltpu.VMEM((bins, 2 * PAIR * rows, parts * lanes), BF16)
    return pl.pallas_call(
        functools.partial(cross_kernel, groups, parts, cuts),
        out_shape=jax.ShapeDtypeStruct((PAIR * bins, 2, rows, groups * PAIR * rows), BF16),
        in_specs=[pl.BlockSpec(memory_space=pl.ANY)],
        out_specs=pl.BlockSpec(memory_space=pltpu.VMEM),
        scratch_shapes=[
            pltpu.VMEM((groups, pieces, bins, rows, lanes), BF16),
            left,
            left,
            pltpu.VMEM((groups, bins, 2, rows, PAIR * rows), BF16),
            pltpu.VMEM((groups, PAIR, bins, 2, rows, PAIR * rows), BF16),
            dma, dma((pieces, cuts)), dma((pieces, cuts)),
            dma((groups, pieces, cuts)), dma((groups, pieces, cuts)), dma((groups, pieces, cuts)),
            dma((groups, cuts)), dma((groups, cuts)),
            dma((groups, PAIR, cuts)), dma((groups, PAIR, cuts)),
        ],
        compiler_params=pltpu.CompilerParams(
            collective_id=0, has_side_effects=True, vmem_limit_bytes=56 * 2**20
        ),
    )(weighted)


def per_device(strain, mad_index, mad_table, freq_bins, valid_count):
    channels, wins, length = strain.shape
    bins = freq_bins.shape[0]
    entries = jnp.arange(mad_table.shape[0], dtype=jnp.int32)
    matches = mad_index[:, None] == entries[None, :]
    limits = jnp.sum(jnp.where(matches, mad_table[None, :], 0.0), axis=1) * CLIP_FACTOR
    roots = 1.0 / jnp.sqrt(valid_count.astype(F32))
    table = dft_rows(freq_bins, length)
    weighted = spectra(strain, limits, valid_count, roots, table)
    parts, groups = lax.axis_size("freq"), lax.axis_size("chan") // PAIR
    pieces = parts * PAIR
    weighted = jnp.transpose(weighted, (1, 0, 2)).reshape(pieces, bins // pieces, channels, 2 * wins)
    return cross(weighted, groups, parts).astype(F32)


def solution(mesh):
    return jax.shard_map(
        per_device,
        mesh=mesh,
        in_specs=(P("chan", "freq", None), P("chan"), P(), P(), P("chan")),
        out_specs=P("freq", None, "chan", None),
        check_vma=False,
    )
```

```python
import functools
import math

import jax
import jax.numpy as jnp
from jax import lax
from jax.experimental import pallas as pl
from jax.experimental.pallas import tpu as pltpu
from jax.sharding import PartitionSpec as P

CLIP_FACTOR = 2.0
MESH = pl.DeviceIdType.MESH
PAIR = 2
BF16 = jnp.bfloat16
F32 = jnp.float32


def dft_rows(freq_bins, length):
    samples = jnp.arange(length, dtype=jnp.int32)
    phase_index = freq_bins[:, None] * samples[None, :] % length
    angle = phase_index.astype(F32) * (2.0 * math.pi / length)
    taper = 0.5 - 0.5 * jnp.cos(samples.astype(F32) * (2.0 * math.pi / length))
    cosine = taper[None, :] * jnp.cos(angle)
    sine = -taper[None, :] * jnp.sin(angle)
    return jnp.concatenate([cosine, sine], axis=0).astype(BF16)


def spectrum_kernel(limit_ref, count_ref, root_ref, table_ref, strain_ref, out_ref):
    block, wins, length = strain_ref.shape
    bins = out_ref.shape[0]
    first = pl.program_id(0) * block
    clipped = []
    for c in range(block):
        limit = jnp.full((wins, 128), limit_ref[first + c], F32).astype(BF16)
        limit = jnp.concatenate([limit] * (length // 128), axis=1)
        clipped.append(jnp.minimum(jnp.maximum(strain_ref[c], -limit), limit))
    rows = jnp.concatenate(clipped, axis=0)
    spectrum = lax.dot_general(
        table_ref[...], rows, (((1,), (1,)), ((), ())), preferred_element_type=F32
    )
    lane = lax.broadcasted_iota(jnp.int32, (bins, 2 * wins), 1)
    low = lane < wins
    window = lax.axis_index("freq") * wins + lax.rem(lane, wins)
    weighted = []
    for c in range(0, block, 2):
        re = spectrum[:bins, c * wins : (c + 2) * wins]
        im = spectrum[bins:, c * wins : (c + 2) * wins]
        even = jnp.where(low, re, pltpu.roll(im, wins, 1))
        odd = jnp.where(low, pltpu.roll(re, wins, 1), im)
        for d, both in enumerate((even, odd)):
            channel = first + c + d
            weight = jnp.where(window < count_ref[channel], root_ref[channel], 0.0)
            weighted.append(both * weight)
    out_ref[...] = jnp.swapaxes(jnp.stack(weighted), 0, 1).astype(BF16)


def spectra(strain, limits, valid_count, roots, table):
    channels, wins, length = strain.shape
    bins = table.shape[0] // 2
    block = 16
    smem = pl.BlockSpec(memory_space=pltpu.SMEM)
    return pl.pallas_call(
        spectrum_kernel,
        grid=(channels // block,),
        out_shape=jax.ShapeDtypeStruct((bins, channels, 2 * wins), BF16),
        in_specs=[
            smem,
            smem,
            smem,
            pl.BlockSpec((2 * bins, length), lambda i: (0, 0)),
            pl.BlockSpec((block, wins, length), lambda i: (i, 0, 0)),
        ],
        out_specs=pl.BlockSpec((bins, block, 2 * wins), lambda i: (0, i, 0)),
        compiler_params=pltpu.CompilerParams(vmem_limit_bytes=32 * 2**20),
    )(limits, valid_count, roots, table, strain)


def cross_kernel(groups, parts, cuts, w_ref, o_ref, panel, left, left_end, stage, stage_end, own_sem, a_send,
                 a_recv, up_send, down_send, z_recv, r_send, r_recv, e_send, e_recv):
    pieces = parts * PAIR
    bins, rows, lanes = panel.shape[2:]
    cut = bins // cuts
    height = PAIR * rows
    half = lanes // 2
    last = groups - 1
    chan, q = lax.axis_index("chan"), lax.axis_index("freq")
    z, x = chan // PAIR, lax.rem(chan, PAIR)
    me = q * PAIR + x
    is_end = (z == 0) | (z == last)
    is_inner = (z > 0) & (z < last)
    low_pair, high_pair = (z == 1), (z == last - 1)
    is_helper = low_pair | high_pair
    end = jnp.where(low_pair, 0, last)
    sends_up, sends_down = z < last - 1, z > 1

    def place(piece):
        return (z * PAIR + lax.rem(piece, PAIR), piece // PAIR)

    def at(group, side):
        return (group * PAIR + side, q)

    above, below, mate = at(z + 1, x), at(z - 1, x), at(z, 1 - x)

    barrier = pltpu.get_barrier_semaphore()

    def greet(device):
        pl.semaphore_signal(barrier, inc=1, device_id=device, device_id_type=MESH)

    for d in range(1, pieces):
        greet(place(lax.rem(me + d, pieces)))

    @pl.when(z < last)
    def _():
        greet(above)

    @pl.when(z > 0)
    def _():
        greet(below)

    @pl.when((z == 0) | high_pair)
    def _():
        greet(at(z + 1, 1 - x))

    @pl.when((z == last) | low_pair)
    def _():
        greet(at(z - 1, 1 - x))

    greeted = pieces - 1 + jnp.where(z < last, 1, 0) + jnp.where(z > 0, 1, 0)
    greeted = greeted + jnp.where(is_end | is_helper, 1, 0)
    pl.semaphore_wait(barrier, greeted)

    def span(h):
        return pl.ds(h * cut, cut)

    def swap(d, h):
        to = lax.rem(me + d, pieces)
        return pltpu.make_async_remote_copy(
            src_ref=w_ref.at[to, span(h)], dst_ref=panel.at[z, me, span(h)], send_sem=a_send.at[d, h],
            recv_sem=a_recv.at[d, h], device_id=place(to), device_id_type=MESH)

    def arrival(d, h):
        source = lax.rem(me + pieces - d, pieces)
        return source, pltpu.make_async_remote_copy(
            src_ref=w_ref.at[source, span(h)], dst_ref=panel.at[z, source, span(h)], send_sem=a_send.at[d, h],
            recv_sem=a_recv.at[d, h], device_id=place(source), device_id_type=MESH)

    def along(p, k, h, sems, target):
        return pltpu.make_async_remote_copy(
            src_ref=panel.at[p, k, span(h)], dst_ref=panel.at[p, k, span(h)], send_sem=sems.at[p, k, h],
            recv_sem=z_recv.at[p, k, h], device_id=target, device_id_type=MESH)

    def pass_up(p, k, h):
        @pl.when(sends_up)
        def _():
            along(p, k, h, up_send, above).start()

    def pass_down(p, k, h):
        @pl.when(sends_down)
        def _():
            along(p, k, h, down_send, below).start()

    own = pltpu.make_async_copy(w_ref.at[me], panel.at[z, me], own_sem)
    own.start()
    for h in range(cuts):
        for d in range(1, pieces):
            swap(d, h).start()
    own.wait()

    def wide(p, f):
        return jnp.concatenate(
            [
                jnp.concatenate([panel[p, part * PAIR + i, f] for i in range(PAIR)], axis=0)
                for part in range(parts)
            ],
            axis=1,
        )

    def make_left(target, p, h):
        @pl.loop(0, cut)
        def _(i):
            f = h * cut + i
            plain = wide(p, f)
            target[f, pl.ds(0, height)] = plain
            sign = jnp.where(lax.broadcasted_iota(jnp.int32, (height, lanes), 1) < half, 1.0, -1.0)
            for part in range(parts):
                turned = pltpu.roll(plain[:, part * lanes : (part + 1) * lanes].astype(F32), half, 1)
                target[f, pl.ds(height, height), pl.ds(part * lanes, lanes)] = (turned * sign).astype(BF16)

    def columns(p):
        return pl.ds(pl.multiple_of(p * height, height), height)

    def give_back(p, h, side):
        return pltpu.make_async_remote_copy(
            src_ref=stage.at[p, span(h)],
            dst_ref=o_ref.at[pl.ds(side * bins + h * cut, cut), :, :, columns(p)],
            send_sem=r_send.at[p, h], recv_sem=r_recv.at[p, h], device_id=mate, device_id_type=MESH)

    def give_end(p, h, to, source):
        return pltpu.make_async_remote_copy(
            src_ref=stage_end.at[p, to, span(h)],
            dst_ref=o_ref.at[pl.ds(source * bins + h * cut, cut), :, :, columns(p)],
            send_sem=e_send.at[p, to, h], recv_sem=e_recv.at[p, source, h],
            device_id=at(end, to), device_id_type=MESH)

    def product_of(lhs, p, f):
        return lax.dot_general(
            lhs[f], wide(p, f), (((1,), (1,)), ((), ())), preferred_element_type=F32
        ).astype(BF16)

    def block(p, h):
        @pl.loop(0, cut)
        def _(i):
            f = h * cut + i
            product = product_of(left, p, f)
            for part in range(2):
                lower = product[part * height : part * height + rows]
                upper = product[part * height + rows : (part + 1) * height]
                o_ref[x * bins + f, part, :, columns(p)] = jnp.where(x == 0, lower, upper)
                stage[p, f, part] = jnp.where(x == 0, upper, lower)

        give_back(p, h, x).start()

    def block_end(p, h):
        @pl.loop(0, cut)
        def _(i):
            f = h * cut + i
            product = product_of(left_end, p, f)
            for part in range(2):
                for to in range(PAIR):
                    top = part * height + to * rows
                    stage_end[p, to, f, part] = product[top : top + rows]

        for to in range(PAIR):
            give_end(p, h, to, x).start()

    for h in range(cuts):
        pass_up(z, me, h)
        pass_down(z, me, h)
    for h in range(cuts):
        for d in range(1, pieces):
            source, copy = arrival(d, h)
            copy.wait_recv()
            pass_up(z, source, h)
            pass_down(z, source, h)
    for h in range(cuts):
        make_left(left, z, h)
        block(z, h)

    def step(s, carry):
        lower, upper = z - 1 - s, z + 1 + s
        for h in range(cuts):
            @pl.when(lower >= 0)
            def _():
                for k in range(pieces):
                    along(lower, k, h, up_send, above).wait_recv()
                    pass_up(lower, k, h)

            @pl.when(upper <= last)
            def _():
                for k in range(pieces):
                    along(upper, k, h, down_send, below).wait_recv()
                    pass_down(upper, k, h)

            @pl.when(is_helper & (s == 0))
            def _():
                make_left(left_end, end, h)
                block_end(z, h)

            @pl.when(is_helper & (lower > 0))
            def _():
                block_end(lower, h)

            @pl.when(is_helper & (upper < last))
            def _():
                block_end(upper, h)

            @pl.when(low_pair & (upper == last))
            def _():
                block_end(upper, h)

            @pl.when(high_pair & (lower == 0))
            def _():
                block_end(lower, h)

            @pl.when(lower >= 0)
            def _():
                block(lower, h)

            @pl.when(upper <= last)
            def _():
                block(upper, h)

        return carry

    @pl.when(is_inner)
    def _():
        lax.fori_loop(0, last, step, 0)

    for h in range(cuts):
        for d in range(1, pieces):
            swap(d, h).wait_send()

    def finish(p, carry):
        for h in range(cuts):
            @pl.when(is_inner | (p == z))
            def _():
                give_back(p, h, x).wait_send()
                give_back(p, h, 1 - x).wait_recv()

            @pl.when(is_end & (p != z))
            def _():
                for source in range(PAIR):
                    give_end(p, h, 0, source).wait_recv()

            @pl.when(is_helper & (p != end))
            def _():
                for to in range(PAIR):
                    give_end(p, h, to, x).wait_send()

            for k in range(pieces):
                @pl.when(sends_up & (p <= z))
                def _():
                    along(p, k, h, up_send, above).wait_send()

                @pl.when(sends_down & (p >= z))
                def _():
                    along(p, k, h, down_send, below).wait_send()

        return carry

    lax.fori_loop(0, groups, finish, 0)


def cross(weighted, groups, parts):
    assert groups >= 4
    pieces, bins, rows, lanes = weighted.shape
    cuts = 4
    dma = pltpu.SemaphoreType.DMA
    left = pltpu.VMEM((bins, 2 * PAIR * rows, parts * lanes), BF16)
    return pl.pallas_call(
        functools.partial(cross_kernel, groups, parts, cuts),
        out_shape=jax.ShapeDtypeStruct((PAIR * bins, 2, rows, groups * PAIR * rows), BF16),
        in_specs=[pl.BlockSpec(memory_space=pl.ANY)],
        out_specs=pl.BlockSpec(memory_space=pltpu.VMEM),
        scratch_shapes=[
            pltpu.VMEM((groups, pieces, bins, rows, lanes), BF16),
            left,
            left,
            pltpu.VMEM((groups, bins, 2, rows, PAIR * rows), BF16),
            pltpu.VMEM((groups, PAIR, bins, 2, rows, PAIR * rows), BF16),
            dma, dma((pieces, cuts)), dma((pieces, cuts)),
            dma((groups, pieces, cuts)), dma((groups, pieces, cuts)), dma((groups, pieces, cuts)),
            dma((groups, cuts)), dma((groups, cuts)),
            dma((groups, PAIR, cuts)), dma((groups, PAIR, cuts)),
        ],
        compiler_params=pltpu.CompilerParams(
            collective_id=0, has_side_effects=True, vmem_limit_bytes=56 * 2**20
        ),
    )(weighted)


def per_device(strain, mad_index, mad_table, freq_bins, valid_count):
    channels, wins, length = strain.shape
    bins = freq_bins.shape[0]
    entries = jnp.arange(mad_table.shape[0], dtype=jnp.int32)
    matches = mad_index[:, None] == entries[None, :]
    limits = jnp.sum(jnp.where(matches, mad_table[None, :], 0.0), axis=1) * CLIP_FACTOR
    roots = 1.0 / jnp.sqrt(valid_count.astype(F32))
    table = dft_rows(freq_bins, length)
    weighted = spectra(strain, limits, valid_count, roots, table)
    parts, groups = lax.axis_size("freq"), lax.axis_size("chan") // PAIR
    pieces = parts * PAIR
    weighted = weighted.reshape(pieces, bins // pieces, channels, 2 * wins)
    return cross(weighted, groups, parts).astype(F32)


def solution(mesh):
    return jax.shard_map(
        per_device,
        mesh=mesh,
        in_specs=(P("chan", "freq", None), P("chan"), P(), P(), P("chan")),
        out_specs=P("freq", None, "chan", None),
        check_vma=False,
    )
```

```python
import functools
import math

import jax
import jax.numpy as jnp
from jax import lax
from jax.experimental import pallas as pl
from jax.experimental.pallas import tpu as pltpu
from jax.sharding import PartitionSpec as P

CLIP_FACTOR = 2.0
MESH = pl.DeviceIdType.MESH
PAIR = 2
BF16 = jnp.bfloat16
F32 = jnp.float32


def dft_rows(freq_bins, length):
    samples = jnp.arange(length, dtype=jnp.int32)
    phase_index = freq_bins[:, None] * samples[None, :] % length
    angle = phase_index.astype(F32) * (2.0 * math.pi / length)
    taper = 0.5 - 0.5 * jnp.cos(samples.astype(F32) * (2.0 * math.pi / length))
    cosine = taper[None, :] * jnp.cos(angle)
    sine = -taper[None, :] * jnp.sin(angle)
    return jnp.concatenate([cosine, sine], axis=0).astype(BF16)


def spectrum_kernel(index_ref, scale_ref, count_ref, table_ref, strain_ref, out_ref):
    block, wins, length = strain_ref.shape
    bins = out_ref.shape[0]
    first = pl.program_id(0) * block
    clipped = []
    for c in range(block):
        limit = jnp.full((wins, 128), scale_ref[index_ref[first + c]] * CLIP_FACTOR, F32).astype(BF16)
        limit = jnp.concatenate([limit] * (length // 128), axis=1)
        clipped.append(jnp.minimum(jnp.maximum(strain_ref[c], -limit), limit))
    rows = jnp.concatenate(clipped, axis=0)
    spectrum = lax.dot_general(
        table_ref[...], rows, (((1,), (1,)), ((), ())), preferred_element_type=F32
    )
    lane = lax.broadcasted_iota(jnp.int32, (bins, 2 * wins), 1)
    low = lane < wins
    window = lax.axis_index("freq") * wins + lax.rem(lane, wins)
    weighted = []
    for c in range(0, block, 2):
        re = spectrum[:bins, c * wins : (c + 2) * wins]
        im = spectrum[bins:, c * wins : (c + 2) * wins]
        even = jnp.where(low, re, pltpu.roll(im, wins, 1))
        odd = jnp.where(low, pltpu.roll(re, wins, 1), im)
        for d, both in enumerate((even, odd)):
            channel = first + c + d
            root = 1.0 / jnp.sqrt(jnp.full((1, 2 * wins), count_ref[channel], jnp.int32).astype(F32))
            weight = jnp.where(window < count_ref[channel], root, 0.0)
            weighted.append(both * weight)
    out_ref[...] = jnp.swapaxes(jnp.stack(weighted), 0, 1).astype(BF16)


def spectra(strain, mad_index, mad_table, valid_count, table):
    channels, wins, length = strain.shape
    bins = table.shape[0] // 2
    block = 16
    smem = pl.BlockSpec(memory_space=pltpu.SMEM)
    return pl.pallas_call(
        spectrum_kernel,
        grid=(channels // block,),
        out_shape=jax.ShapeDtypeStruct((bins, channels, 2 * wins), BF16),
        in_specs=[
            smem,
            smem,
            smem,
            pl.BlockSpec((2 * bins, length), lambda i: (0, 0)),
            pl.BlockSpec((block, wins, length), lambda i: (i, 0, 0)),
        ],
        out_specs=pl.BlockSpec((bins, block, 2 * wins), lambda i: (0, i, 0)),
        compiler_params=pltpu.CompilerParams(vmem_limit_bytes=32 * 2**20),
    )(mad_index, mad_table, valid_count, table, strain)


def cross_kernel(groups, parts, cuts, w_ref, o_ref, panel, left, left_end, stage, stage_end, own_sem, a_send,
                 a_recv, up_send, down_send, z_recv, r_send, r_recv, e_send, e_recv):
    pieces = parts * PAIR
    bins, rows, lanes = panel.shape[2:]
    cut = bins // cuts
    height = PAIR * rows
    half = lanes // 2
    last = groups - 1
    chan, q = lax.axis_index("chan"), lax.axis_index("freq")
    z, x = chan // PAIR, lax.rem(chan, PAIR)
    me = q * PAIR + x
    is_end = (z == 0) | (z == last)
    is_inner = (z > 0) & (z < last)
    low_pair, high_pair = (z == 1), (z == last - 1)
    is_helper = low_pair | high_pair
    end = jnp.where(low_pair, 0, last)
    sends_up, sends_down = z < last - 1, z > 1

    def place(piece):
        return (z * PAIR + lax.rem(piece, PAIR), piece // PAIR)

    def at(group, side):
        return (group * PAIR + side, q)

    above, below, mate = at(z + 1, x), at(z - 1, x), at(z, 1 - x)

    barrier = pltpu.get_barrier_semaphore()

    def greet(device):
        pl.semaphore_signal(barrier, inc=1, device_id=device, device_id_type=MESH)

    for d in range(1, pieces):
        greet(place(lax.rem(me + d, pieces)))

    @pl.when(z < last)
    def _():
        greet(above)

    @pl.when(z > 0)
    def _():
        greet(below)

    @pl.when((z == 0) | high_pair)
    def _():
        greet(at(z + 1, 1 - x))

    @pl.when((z == last) | low_pair)
    def _():
        greet(at(z - 1, 1 - x))

    greeted = pieces - 1 + jnp.where(z < last, 1, 0) + jnp.where(z > 0, 1, 0)
    greeted = greeted + jnp.where(is_end | is_helper, 1, 0)
    pl.semaphore_wait(barrier, greeted)

    def span(h):
        return pl.ds(h * cut, cut)

    def swap(d, h):
        to = lax.rem(me + d, pieces)
        return pltpu.make_async_remote_copy(
            src_ref=w_ref.at[to, span(h)], dst_ref=panel.at[z, me, span(h)], send_sem=a_send.at[d, h],
            recv_sem=a_recv.at[d, h], device_id=place(to), device_id_type=MESH)

    def arrival(d, h):
        source = lax.rem(me + pieces - d, pieces)
        return source, pltpu.make_async_remote_copy(
            src_ref=w_ref.at[source, span(h)], dst_ref=panel.at[z, source, span(h)], send_sem=a_send.at[d, h],
            recv_sem=a_recv.at[d, h], device_id=place(source), device_id_type=MESH)

    def along(p, k, h, sems, target):
        return pltpu.make_async_remote_copy(
            src_ref=panel.at[p, k, span(h)], dst_ref=panel.at[p, k, span(h)], send_sem=sems.at[p, k, h],
            recv_sem=z_recv.at[p, k, h], device_id=target, device_id_type=MESH)

    def pass_up(p, k, h):
        @pl.when(sends_up)
        def _():
            along(p, k, h, up_send, above).start()

    def pass_down(p, k, h):
        @pl.when(sends_down)
        def _():
            along(p, k, h, down_send, below).start()

    own = pltpu.make_async_copy(w_ref.at[me], panel.at[z, me], own_sem)
    own.start()
    for h in range(cuts):
        for d in range(1, pieces):
            swap(d, h).start()
    own.wait()

    def wide(p, f):
        return jnp.concatenate(
            [
                jnp.concatenate([panel[p, part * PAIR + i, f] for i in range(PAIR)], axis=0)
                for part in range(parts)
            ],
            axis=1,
        )

    def make_left(target, p, h):
        @pl.loop(0, cut)
        def _(i):
            f = h * cut + i
            plain = wide(p, f)
            target[f, pl.ds(0, height)] = plain
            sign = jnp.where(lax.broadcasted_iota(jnp.int32, (height, lanes), 1) < half, 1.0, -1.0)
            for part in range(parts):
                turned = pltpu.roll(plain[:, part * lanes : (part + 1) * lanes].astype(F32), half, 1)
                target[f, pl.ds(height, height), pl.ds(part * lanes, lanes)] = (turned * sign).astype(BF16)

    def columns(p):
        return pl.ds(pl.multiple_of(p * height, height), height)

    def give_back(p, h, side):
        return pltpu.make_async_remote_copy(
            src_ref=stage.at[p, span(h)],
            dst_ref=o_ref.at[pl.ds(side * bins + h * cut, cut), :, :, columns(p)],
            send_sem=r_send.at[p, h], recv_sem=r_recv.at[p, h], device_id=mate, device_id_type=MESH)

    def give_end(p, h, to, source):
        return pltpu.make_async_remote_copy(
            src_ref=stage_end.at[p, to, span(h)],
            dst_ref=o_ref.at[pl.ds(source * bins + h * cut, cut), :, :, columns(p)],
            send_sem=e_send.at[p, to, h], recv_sem=e_recv.at[p, source, h],
            device_id=at(end, to), device_id_type=MESH)

    def product_of(lhs, p, f):
        return lax.dot_general(
            lhs[f], wide(p, f), (((1,), (1,)), ((), ())), preferred_element_type=F32
        ).astype(BF16)

    def block(p, h):
        @pl.loop(0, cut)
        def _(i):
            f = h * cut + i
            product = product_of(left, p, f)
            for part in range(2):
                lower = product[part * height : part * height + rows]
                upper = product[part * height + rows : (part + 1) * height]
                o_ref[x * bins + f, part, :, columns(p)] = jnp.where(x == 0, lower, upper)
                stage[p, f, part] = jnp.where(x == 0, upper, lower)

        give_back(p, h, x).start()

    def block_end(p, h):
        @pl.loop(0, cut)
        def _(i):
            f = h * cut + i
            product = product_of(left_end, p, f)
            for part in range(2):
                for to in range(PAIR):
                    top = part * height + to * rows
                    stage_end[p, to, f, part] = product[top : top + rows]

        for to in range(PAIR):
            give_end(p, h, to, x).start()

    for h in range(cuts):
        pass_up(z, me, h)
        pass_down(z, me, h)
    for h in range(cuts):
        for d in range(1, pieces):
            source, copy = arrival(d, h)
            copy.wait_recv()
            pass_up(z, source, h)
            pass_down(z, source, h)
    for h in range(cuts):
        make_left(left, z, h)
        block(z, h)

    def step(s, carry):
        lower, upper = z - 1 - s, z + 1 + s
        in_low_half = z * 2 < groups

        def take_low(h, wanted):
            @pl.when(wanted & (lower >= 0))
            def _():
                for k in range(pieces):
                    along(lower, k, h, up_send, above).wait_recv()
                    pass_up(lower, k, h)

        def take_high(h, wanted):
            @pl.when(wanted & (upper <= last))
            def _():
                for k in range(pieces):
                    along(upper, k, h, down_send, below).wait_recv()
                    pass_down(upper, k, h)

        def take_near(h):
            take_low(h, in_low_half)
            take_high(h, z * 2 >= groups)

        def take_far(h):
            take_high(h, in_low_half)
            take_low(h, z * 2 >= groups)

        take_near(0)
        for h in range(cuts):
            if h + 1 < cuts:
                take_near(h + 1)
            take_far(h)

            @pl.when(is_helper & (s == 0))
            def _():
                make_left(left_end, end, h)
                block_end(z, h)

            @pl.when(is_helper & (lower > 0))
            def _():
                block_end(lower, h)

            @pl.when(is_helper & (upper < last))
            def _():
                block_end(upper, h)

            @pl.when(low_pair & (upper == last))
            def _():
                block_end(upper, h)

            @pl.when(high_pair & (lower == 0))
            def _():
                block_end(lower, h)

            @pl.when(lower >= 0)
            def _():
                block(lower, h)

            @pl.when(upper <= last)
            def _():
                block(upper, h)

        return carry

    @pl.when(is_inner)
    def _():
        lax.fori_loop(0, last, step, 0)

    for h in range(cuts):
        for d in range(1, pieces):
            swap(d, h).wait_send()

    def finish(p, carry):
        for h in range(cuts):
            @pl.when(is_inner | (p == z))
            def _():
                give_back(p, h, x).wait_send()
                give_back(p, h, 1 - x).wait_recv()

            @pl.when(is_end & (p != z))
            def _():
                for source in range(PAIR):
                    give_end(p, h, 0, source).wait_recv()

            @pl.when(is_helper & (p != end))
            def _():
                for to in range(PAIR):
                    give_end(p, h, to, x).wait_send()

            for k in range(pieces):
                @pl.when(sends_up & (p <= z))
                def _():
                    along(p, k, h, up_send, above).wait_send()

                @pl.when(sends_down & (p >= z))
                def _():
                    along(p, k, h, down_send, below).wait_send()

        return carry

    lax.fori_loop(0, groups, finish, 0)


def cross(weighted, groups, parts):
    assert groups >= 4
    pieces, bins, rows, lanes = weighted.shape
    cuts = 4
    dma = pltpu.SemaphoreType.DMA
    left = pltpu.VMEM((bins, 2 * PAIR * rows, parts * lanes), BF16)
    return pl.pallas_call(
        functools.partial(cross_kernel, groups, parts, cuts),
        out_shape=jax.ShapeDtypeStruct((PAIR * bins, 2, rows, groups * PAIR * rows), BF16),
        in_specs=[pl.BlockSpec(memory_space=pl.ANY)],
        out_specs=pl.BlockSpec(memory_space=pltpu.VMEM),
        scratch_shapes=[
            pltpu.VMEM((groups, pieces, bins, rows, lanes), BF16),
            left,
            left,
            pltpu.VMEM((groups, bins, 2, rows, PAIR * rows), BF16),
            pltpu.VMEM((groups, PAIR, bins, 2, rows, PAIR * rows), BF16),
            dma, dma((pieces, cuts)), dma((pieces, cuts)),
            dma((groups, pieces, cuts)), dma((groups, pieces, cuts)), dma((groups, pieces, cuts)),
            dma((groups, cuts)), dma((groups, cuts)),
            dma((groups, PAIR, cuts)), dma((groups, PAIR, cuts)),
        ],
        compiler_params=pltpu.CompilerParams(
            collective_id=0, has_side_effects=True, vmem_limit_bytes=56 * 2**20
        ),
    )(weighted)


def per_device(strain, mad_index, mad_table, freq_bins, valid_count):
    channels, wins, length = strain.shape
    bins = freq_bins.shape[0]
    table = dft_rows(freq_bins, length)
    weighted = spectra(strain, mad_index, mad_table, valid_count, table)
    parts, groups = lax.axis_size("freq"), lax.axis_size("chan") // PAIR
    pieces = parts * PAIR
    weighted = weighted.reshape(pieces, bins // pieces, channels, 2 * wins)
    return cross(weighted, groups, parts).astype(F32)


def solution(mesh):
    return jax.shard_map(
        per_device,
        mesh=mesh,
        in_specs=(P("chan", "freq", None), P("chan"), P(), P(), P("chan")),
        out_specs=P("freq", None, "chan", None),
        check_vma=False,
    )
```

```python
import functools
import math

import jax
import jax.numpy as jnp
from jax import lax
from jax.experimental import pallas as pl
from jax.experimental.pallas import tpu as pltpu
from jax.sharding import PartitionSpec as P

CLIP_FACTOR = 2.0
MESH = pl.DeviceIdType.MESH
PAIR = 2
BF16 = jnp.bfloat16
F32 = jnp.float32


def dft_rows(freq_bins, length):
    samples = jnp.arange(length, dtype=jnp.int32)
    phase_index = freq_bins[:, None] * samples[None, :] % length
    angle = phase_index.astype(F32) * (2.0 * math.pi / length)
    taper = 0.5 - 0.5 * jnp.cos(samples.astype(F32) * (2.0 * math.pi / length))
    cosine = taper[None, :] * jnp.cos(angle)
    sine = -taper[None, :] * jnp.sin(angle)
    return jnp.concatenate([cosine, sine], axis=0).astype(BF16)


def spectrum_kernel(facts_ref, table_ref, strain_ref, out_ref):
    block, wins, length = strain_ref.shape
    bins = out_ref.shape[0]
    first = pl.program_id(0) * block
    clipped = []
    for c in range(block):
        limit = jnp.full((wins, 128), facts_ref[0, first + c], F32).astype(BF16)
        limit = jnp.concatenate([limit] * (length // 128), axis=1)
        clipped.append(jnp.minimum(jnp.maximum(strain_ref[c], -limit), limit))
    rows = jnp.concatenate(clipped, axis=0)
    spectrum = lax.dot_general(
        table_ref[...], rows, (((1,), (1,)), ((), ())), preferred_element_type=F32
    )
    lane = lax.broadcasted_iota(jnp.int32, (bins, 2 * wins), 1)
    low = lane < wins
    window = lax.axis_index("freq") * wins + lax.rem(lane, wins)
    window = window.astype(F32)
    weighted = []
    for c in range(0, block, 2):
        re = spectrum[:bins, c * wins : (c + 2) * wins]
        im = spectrum[bins:, c * wins : (c + 2) * wins]
        even = jnp.where(low, re, pltpu.roll(im, wins, 1))
        odd = jnp.where(low, pltpu.roll(re, wins, 1), im)
        for d, both in enumerate((even, odd)):
            channel = first + c + d
            root = 1.0 / jnp.sqrt(jnp.full((1, 2 * wins), facts_ref[1, channel], F32))
            weight = jnp.where(window < facts_ref[1, channel], root, 0.0)
            weighted.append(both * weight)
    out_ref[...] = jnp.swapaxes(jnp.stack(weighted), 0, 1).astype(BF16)


def spectra(strain, facts, table):
    channels, wins, length = strain.shape
    bins = table.shape[0] // 2
    block = 16
    smem = pl.BlockSpec(memory_space=pltpu.SMEM)
    return pl.pallas_call(
        spectrum_kernel,
        grid=(channels // block,),
        out_shape=jax.ShapeDtypeStruct((bins, channels, 2 * wins), BF16),
        in_specs=[
            smem,
            pl.BlockSpec((2 * bins, length), lambda i: (0, 0)),
            pl.BlockSpec((block, wins, length), lambda i: (i, 0, 0)),
        ],
        out_specs=pl.BlockSpec((bins, block, 2 * wins), lambda i: (0, i, 0)),
        compiler_params=pltpu.CompilerParams(vmem_limit_bytes=32 * 2**20),
    )(facts, table, strain)


def cross_kernel(groups, parts, cuts, w_ref, o_ref, panel, left, left_end, stage, stage_end, own_sem, a_send,
                 a_recv, up_send, down_send, z_recv, r_send, r_recv, e_send, e_recv):
    pieces = parts * PAIR
    bins, rows, lanes = panel.shape[2:]
    cut = bins // cuts
    height = PAIR * rows
    half = lanes // 2
    last = groups - 1
    chan, q = lax.axis_index("chan"), lax.axis_index("freq")
    z, x = chan // PAIR, lax.rem(chan, PAIR)
    me = q * PAIR + x
    is_end = (z == 0) | (z == last)
    is_inner = (z > 0) & (z < last)
    low_pair, high_pair = (z == 1), (z == last - 1)
    is_helper = low_pair | high_pair
    end = jnp.where(low_pair, 0, last)
    sends_up, sends_down = z < last - 1, z > 1

    def place(piece):
        return (z * PAIR + lax.rem(piece, PAIR), piece // PAIR)

    def at(group, side):
        return (group * PAIR + side, q)

    above, below, mate = at(z + 1, x), at(z - 1, x), at(z, 1 - x)

    barrier = pltpu.get_barrier_semaphore()

    def greet(device):
        pl.semaphore_signal(barrier, inc=1, device_id=device, device_id_type=MESH)

    for d in range(1, pieces):
        greet(place(lax.rem(me + d, pieces)))

    @pl.when(z < last)
    def _():
        greet(above)

    @pl.when(z > 0)
    def _():
        greet(below)

    @pl.when((z == 0) | high_pair)
    def _():
        greet(at(z + 1, 1 - x))

    @pl.when((z == last) | low_pair)
    def _():
        greet(at(z - 1, 1 - x))

    greeted = pieces - 1 + jnp.where(z < last, 1, 0) + jnp.where(z > 0, 1, 0)
    greeted = greeted + jnp.where(is_end | is_helper, 1, 0)
    pl.semaphore_wait(barrier, greeted)

    def span(h):
        return pl.ds(h * cut, cut)

    def swap(d, h):
        to = lax.rem(me + d, pieces)
        return pltpu.make_async_remote_copy(
            src_ref=w_ref.at[to, span(h)], dst_ref=panel.at[z, me, span(h)], send_sem=a_send.at[d, h],
            recv_sem=a_recv.at[d, h], device_id=place(to), device_id_type=MESH)

    def arrival(d, h):
        source = lax.rem(me + pieces - d, pieces)
        return source, pltpu.make_async_remote_copy(
            src_ref=w_ref.at[source, span(h)], dst_ref=panel.at[z, source, span(h)], send_sem=a_send.at[d, h],
            recv_sem=a_recv.at[d, h], device_id=place(source), device_id_type=MESH)

    def along(p, k, h, sems, target):
        return pltpu.make_async_remote_copy(
            src_ref=panel.at[p, k, span(h)], dst_ref=panel.at[p, k, span(h)], send_sem=sems.at[p, k, h],
            recv_sem=z_recv.at[p, k, h], device_id=target, device_id_type=MESH)

    def pass_up(p, k, h):
        @pl.when(sends_up)
        def _():
            along(p, k, h, up_send, above).start()

    def pass_down(p, k, h):
        @pl.when(sends_down)
        def _():
            along(p, k, h, down_send, below).start()

    own = pltpu.make_async_copy(w_ref.at[me], panel.at[z, me], own_sem)
    own.start()
    for h in range(cuts):
        for d in range(1, pieces):
            swap(d, h).start()
    own.wait()

    def wide(p, f):
        return jnp.concatenate(
            [
                jnp.concatenate([panel[p, part * PAIR + i, f] for i in range(PAIR)], axis=0)
                for part in range(parts)
            ],
            axis=1,
        )

    def make_left(target, p, h):
        @pl.loop(0, cut)
        def _(i):
            f = h * cut + i
            plain = wide(p, f)
            target[f, pl.ds(0, height)] = plain
            sign = jnp.where(lax.broadcasted_iota(jnp.int32, (height, lanes), 1) < half, 1.0, -1.0)
            for part in range(parts):
                turned = pltpu.roll(plain[:, part * lanes : (part + 1) * lanes].astype(F32), half, 1)
                target[f, pl.ds(height, height), pl.ds(part * lanes, lanes)] = (turned * sign).astype(BF16)

    def columns(p):
        return pl.ds(pl.multiple_of(p * height, height), height)

    def give_back(p, h, side):
        return pltpu.make_async_remote_copy(
            src_ref=stage.at[p, span(h)],
            dst_ref=o_ref.at[pl.ds(side * bins + h * cut, cut), :, :, columns(p)],
            send_sem=r_send.at[p, h], recv_sem=r_recv.at[p, h], device_id=mate, device_id_type=MESH)

    def give_end(p, h, to, source):
        return pltpu.make_async_remote_copy(
            src_ref=stage_end.at[p, to, span(h)],
            dst_ref=o_ref.at[pl.ds(source * bins + h * cut, cut), :, :, columns(p)],
            send_sem=e_send.at[p, to, h], recv_sem=e_recv.at[p, source, h],
            device_id=at(end, to), device_id_type=MESH)

    def product_of(lhs, p, f):
        return lax.dot_general(
            lhs[f], wide(p, f), (((1,), (1,)), ((), ())), preferred_element_type=F32
        ).astype(BF16)

    def block(p, h):
        @pl.loop(0, cut)
        def _(i):
            f = h * cut + i
            product = product_of(left, p, f)
            for part in range(2):
                lower = product[part * height : part * height + rows]
                upper = product[part * height + rows : (part + 1) * height]
                o_ref[x * bins + f, part, :, columns(p)] = jnp.where(x == 0, lower, upper)
                stage[p, f, part] = jnp.where(x == 0, upper, lower)

        give_back(p, h, x).start()

    def block_end(p, h):
        @pl.loop(0, cut)
        def _(i):
            f = h * cut + i
            product = product_of(left_end, p, f)
            for part in range(2):
                for to in range(PAIR):
                    top = part * height + to * rows
                    stage_end[p, to, f, part] = product[top : top + rows]

        for to in range(PAIR):
            give_end(p, h, to, x).start()

    for h in range(cuts):
        pass_up(z, me, h)
        pass_down(z, me, h)
    for h in range(cuts):
        for d in range(1, pieces):
            source, copy = arrival(d, h)
            copy.wait_recv()
            pass_up(z, source, h)
            pass_down(z, source, h)
    for h in range(cuts):
        make_left(left, z, h)
        block(z, h)

    def step(s, carry):
        lower, upper = z - 1 - s, z + 1 + s
        in_low_half = z * 2 < groups

        def take_low(h, wanted):
            @pl.when(wanted & (lower >= 0))
            def _():
                for k in range(pieces):
                    along(lower, k, h, up_send, above).wait_recv()
                    pass_up(lower, k, h)

        def take_high(h, wanted):
            @pl.when(wanted & (upper <= last))
            def _():
                for k in range(pieces):
                    along(upper, k, h, down_send, below).wait_recv()
                    pass_down(upper, k, h)

        def take_near(h):
            take_low(h, in_low_half)
            take_high(h, z * 2 >= groups)

        def take_far(h):
            take_high(h, in_low_half)
            take_low(h, z * 2 >= groups)

        take_near(0)
        for h in range(cuts):
            if h + 1 < cuts:
                take_near(h + 1)
            take_far(h)

            @pl.when(is_helper & (s == 0))
            def _():
                make_left(left_end, end, h)
                block_end(z, h)

            @pl.when(is_helper & (lower > 0))
            def _():
                block_end(lower, h)

            @pl.when(is_helper & (upper < last))
            def _():
                block_end(upper, h)

            @pl.when(low_pair & (upper == last))
            def _():
                block_end(upper, h)

            @pl.when(high_pair & (lower == 0))
            def _():
                block_end(lower, h)

            @pl.when(lower >= 0)
            def _():
                block(lower, h)

            @pl.when(upper <= last)
            def _():
                block(upper, h)

        return carry

    @pl.when(is_inner)
    def _():
        lax.fori_loop(0, last, step, 0)

    for h in range(cuts):
        for d in range(1, pieces):
            swap(d, h).wait_send()

    def finish(p, carry):
        for h in range(cuts):
            @pl.when(is_inner | (p == z))
            def _():
                give_back(p, h, x).wait_send()
                give_back(p, h, 1 - x).wait_recv()

            @pl.when(is_end & (p != z))
            def _():
                for source in range(PAIR):
                    give_end(p, h, 0, source).wait_recv()

            @pl.when(is_helper & (p != end))
            def _():
                for to in range(PAIR):
                    give_end(p, h, to, x).wait_send()

            for k in range(pieces):
                @pl.when(sends_up & (p <= z))
                def _():
                    along(p, k, h, up_send, above).wait_send()

                @pl.when(sends_down & (p >= z))
                def _():
                    along(p, k, h, down_send, below).wait_send()

        return carry

    lax.fori_loop(0, groups, finish, 0)


def cross(weighted, groups, parts):
    assert groups >= 4
    pieces, bins, rows, lanes = weighted.shape
    cuts = 4
    dma = pltpu.SemaphoreType.DMA
    left = pltpu.VMEM((bins, 2 * PAIR * rows, parts * lanes), BF16)
    return pl.pallas_call(
        functools.partial(cross_kernel, groups, parts, cuts),
        out_shape=jax.ShapeDtypeStruct((PAIR * bins, 2, rows, groups * PAIR * rows), BF16),
        in_specs=[pl.BlockSpec(memory_space=pltpu.VMEM)],
        out_specs=pl.BlockSpec(memory_space=pltpu.VMEM),
        scratch_shapes=[
            pltpu.VMEM((groups, pieces, bins, rows, lanes), BF16),
            left,
            left,
            pltpu.VMEM((groups, bins, 2, rows, PAIR * rows), BF16),
            pltpu.VMEM((groups, PAIR, bins, 2, rows, PAIR * rows), BF16),
            dma, dma((pieces, cuts)), dma((pieces, cuts)),
            dma((groups, pieces, cuts)), dma((groups, pieces, cuts)), dma((groups, pieces, cuts)),
            dma((groups, cuts)), dma((groups, cuts)),
            dma((groups, PAIR, cuts)), dma((groups, PAIR, cuts)),
        ],
        compiler_params=pltpu.CompilerParams(
            collective_id=0, has_side_effects=True, vmem_limit_bytes=(3 * groups + 12) * 2**20
        ),
    )(weighted)


def per_device(strain, mad_index, mad_table, freq_bins, valid_count):
    channels, wins, length = strain.shape
    bins = freq_bins.shape[0]
    table = dft_rows(freq_bins, length)
    entries = jnp.arange(mad_table.shape[0], dtype=jnp.int32)
    matches = mad_index[:, None] == entries[None, :]
    limits = jnp.sum(jnp.where(matches, mad_table[None, :], 0.0), axis=1) * CLIP_FACTOR
    facts = jnp.stack([limits, valid_count.astype(F32)])
    weighted = spectra(strain, facts, table)
    parts, groups = lax.axis_size("freq"), lax.axis_size("chan") // PAIR
    pieces = parts * PAIR
    weighted = weighted.reshape(pieces, bins // pieces, channels, 2 * wins)
    return cross(weighted, groups, parts).astype(F32)


def solution(mesh):
    return jax.shard_map(
        per_device,
        mesh=mesh,
        in_specs=(P("chan", "freq", None), P("chan"), P(), P(), P("chan")),
        out_specs=P("freq", None, "chan", None),
        check_vma=False,
    )
```
